32 devices in a mesh: exp: 16 (over z, y, core), feat: 2 (over x).
Axes of the slice: x: 2, y: 2, z: 4, core: 2. Of those that a mesh axis runs over, the one named last changes fastest.
Arguments:
- tokens: bfloat16 [256, 7168], P('exp', 'feat'), may hold values from -6 to 6
- route_ids: int32 [256, 8], P('exp'), may hold values from 0 to 15, all different within a row
- route_weights: float32 [256, 8], P('exp'), may hold values from 0.05 to 0.6
- gate_proj: bfloat16 [16, 7168, 1024], P('exp', 'feat'), may hold values from -0.0625 to 0.0625
- up_proj: bfloat16 [16, 7168, 1024], P('exp', 'feat'), may hold values from -0.0625 to 0.0625
- down_proj: bfloat16 [16, 1024, 7168], P('exp', None, 'feat'), may hold values from -0.1875 to 0.1875
- enc_weight: bfloat16 [7168, 65536], P('feat', 'exp'), may hold values from -0.0625 to 0.0625
- enc_bias: float32 [65536], P('exp'), may hold values from -3 to 3
- dec_weight: bfloat16 [65536, 7168], P('exp', 'feat'), may hold values from -0.0234375 to 0.0234375
- dec_bias: float32 [7168], P('feat'), may hold values from -3 to 3
- clamp_ids: int32 [64], replicated, may hold values from 0 to 65535, as said below
- clamp_values: bfloat16 [64], replicated, may hold values from 8 to 30
Outputs:
- error_term: float32 [256, 7168], P('exp', 'feat')
- steered: float32 [256, 7168], P('exp', 'feat')
The draws below stay inside these ranges and needn't reach their ends.
Inputs may be any that keep to these rules, and one draw needn't show every extreme that they name: `route_ids`: each token names 8 different experts. `clamp_ids`: 64 different features.
All inputs are finite; a program needn't handle non-finite values.
Results may differ from the reference program's by a relative error of at most 0.0035.
Values may be sent and summed in bfloat16 or wider, within the bound.
No kernel may reach another device: no remote copies, remote signals or barrier semaphores. Data moves between devices by JAX's collectives and lax.ppermute only.
A program may use at most 128 MiB of HBM per device.

```python
import jax
import jax.numpy as jnp
from jax import lax

D = 7168
EFF = 1024
FEATS = 65536
TOP = 8
SLOT = 8
CLAMPS = 64
TOK_DEV = 16
EXPERTS = 16
TOKENS = 256
CAP = 128


def draw_clamp_ids(key, part):
    middle = jax.random.permutation(jax.random.fold_in(key, 1), FEATS - 2)[:CLAMPS - 2].astype(jnp.int32) + 1
    extremes = jnp.array([0, FEATS - 1], dtype=jnp.int32)
    joined = jnp.concatenate([middle, extremes])
    shuffle_order = jax.random.permutation(jax.random.fold_in(key, 2), CLAMPS)
    return joined[shuffle_order].astype(jnp.int32)


def levels(stream_key, extent, pieces, least, high):
    def one(position, parts):
        draws = jax.random.uniform(jax.random.fold_in(jax.random.fold_in(stream_key, 6), position), (parts,), jnp.float32, least / len(pieces), high / len(pieces))
        return jnp.repeat(jnp.exp(draws), extent[position] // parts).reshape((-1,) + (1,) * (len(extent) - position - 1))

    level = one(*pieces[0])
    for cut in pieces[1:]:
        level = level * one(*cut)
    return level


def picks_of(rng, rows, amount, top, lift):
    ranking = jax.random.permutation(jax.random.fold_in(rng, 1), amount)
    boost = ranking
    for power in range(3):
        boost = boost * boost // amount
    boost = boost * lift // amount
    lots = jax.random.randint(jax.random.fold_in(rng, 2), (rows, amount), 0, 4096) + boost
    fixed_rows = jax.random.permutation(jax.random.fold_in(rng, 3), rows)[jnp.arange(amount) % rows]
    lots = jnp.where(jnp.arange(rows)[:, None] == fixed_rows[None, :], 1 << 14, lots)
    score = lots * amount + jnp.arange(amount)
    return lax.top_k(score.astype(jnp.int32), top)[1].astype(jnp.int32)


def gaussian(own_key, extent, scale, limit, shards=(), held_as=jnp.bfloat16):
    values = scale * jax.random.normal(own_key, extent, jnp.float32)
    if shards:
        values = values * levels(own_key, extent, shards, -0.22, 0.18)
    return jnp.clip(values, -limit, limit).astype(held_as)


def setup_inputs(seed: int = 0) -> dict:
    seeds = jax.random.split(jax.random.key(seed), 13)
    return {
        "tokens": gaussian(seeds[0], (TOKENS, D), 1.0, 6.0, ((0, 16), (1, 2))),
        "route_ids": picks_of(seeds[1], TOKENS, EXPERTS, TOP, 8192),
        "route_weights": jnp.clip(0.05 + 0.55 * jax.random.uniform(seeds[2], (TOKENS, TOP), jnp.float32) ** levels(seeds[2], (TOKENS, TOP), ((0, 16),), -0.2, 0.2), 0.05, 0.6),
        "gate_proj": gaussian(seeds[3], (EXPERTS, D, EFF), D ** -0.5, 0.0625, ((0, 16), (1, 2))),
        "up_proj": gaussian(seeds[4], (EXPERTS, D, EFF), D ** -0.5, 0.0625, ((0, 16), (1, 2))),
        "down_proj": gaussian(seeds[5], (EXPERTS, EFF, D), EFF ** -0.5, 0.1875, ((0, 16), (2, 2))),
        "enc_weight": gaussian(seeds[6], (D, FEATS), D ** -0.5, 0.0625, ((0, 2), (1, 16))),
        "enc_bias": gaussian(seeds[7], (FEATS,), 0.5, 3.0, ((0, 16),), jnp.float32),
        "dec_weight": gaussian(seeds[8], (FEATS, D), FEATS ** -0.5, 0.0234375, ((0, 16), (1, 2))),
        "dec_bias": gaussian(seeds[9], (D,), 0.5, 3.0, ((0, 2),), jnp.float32),
        "clamp_ids": draw_clamp_ids(jax.random.fold_in(seeds[12], 71), 0),
        "clamp_values": jnp.clip(jax.random.uniform(seeds[11], (CLAMPS,), jnp.float32, 8.0, 30.0), 8.0, 30.0).astype(jnp.bfloat16),
    }


def route_codes(route_ids):
    total_rows = route_ids.shape[0]
    blocks = total_rows // TOK_DEV
    entries = route_ids.reshape(blocks, TOK_DEV * TOP)
    experts = jnp.arange(EXPERTS, dtype=jnp.int32)
    onehot = (entries[:, :, None] == experts[None, None, :]).astype(jnp.int32)
    before = jnp.sum(jnp.cumsum(onehot, axis=1) * onehot, axis=2) - 1
    retained = before < SLOT
    block_base = (jnp.arange(blocks, dtype=jnp.int32) * SLOT)[:, None]
    slot_code = jnp.where(retained, entries * CAP + block_base + before, EXPERTS * CAP)
    return slot_code.reshape(total_rows, TOP).astype(jnp.int32), retained.reshape(total_rows, TOP)


def one_expert(operands):
    rows_in, gate_w, up_w, down_w = operands
    gate_val = jnp.dot(rows_in, gate_w, preferred_element_type=jnp.float32)
    up_val = jnp.dot(rows_in, up_w, preferred_element_type=jnp.float32)
    hidden = (jax.nn.silu(gate_val) * up_val).astype(jnp.bfloat16)
    return jnp.dot(hidden, down_w, preferred_element_type=jnp.float32).astype(jnp.bfloat16)


def reference(tokens, route_ids, route_weights, gate_proj, up_proj, down_proj, enc_weight, enc_bias, dec_weight, dec_bias, clamp_ids, clamp_values):
    slot_code, retained = route_codes(route_ids)
    flat_code = slot_code.reshape(-1)
    repeated = jnp.repeat(tokens, TOP, axis=0)
    buffers = jnp.zeros((EXPERTS * CAP, D), jnp.bfloat16).at[flat_code].set(repeated, mode="drop")
    buffers = buffers.reshape(EXPERTS, CAP, D)
    expert_out = lax.map(one_expert, (buffers, gate_proj, up_proj, down_proj)).reshape(EXPERTS * CAP, D)
    safe_code = jnp.minimum(flat_code, EXPERTS * CAP - 1).astype(jnp.int32)
    picked = jnp.take(expert_out, safe_code, axis=0).astype(jnp.float32).reshape(TOKENS, TOP, D)
    scales = jnp.where(retained, route_weights, 0.0)
    moe_out = jnp.sum(picked * scales[:, :, None], axis=1)
    pre_act = jnp.dot(tokens, enc_weight, preferred_element_type=jnp.float32) + enc_bias
    feature_act = jax.nn.relu(pre_act).astype(jnp.bfloat16)
    rebuilt = jnp.dot(feature_act, dec_weight, preferred_element_type=jnp.float32)
    chosen = jnp.take(feature_act, clamp_ids, axis=1).astype(jnp.float32)
    change = clamp_values.astype(jnp.float32)[None, :] - chosen
    rows_dec = jnp.take(dec_weight, clamp_ids, axis=0).astype(jnp.float32)
    clamp_shift = jnp.dot(change, rows_dec, precision=lax.Precision.HIGHEST)
    error_term = (moe_out - rebuilt - dec_bias).astype(jnp.float32)
    steered = (moe_out + clamp_shift).astype(jnp.float32)
    return error_term, steered
```

```python
import jax
import jax.numpy as jnp
from jax import lax
from jax.experimental import pallas as pl
from jax.experimental.pallas import tpu as pltpu
from jax.sharding import PartitionSpec as P

SLOT = 8
HALVES = 2
CHUNKS = 4
PIECES = 2
LANES = 128
GROUP = 16


def swap(x, axis, mask):
    size = lax.axis_size(axis)
    return lax.ppermute(x, axis, [(i, i ^ mask) for i in range(size)])


def doublings(size):
    masks = []
    while size > 1:
        size //= 2
        masks.append(size)
    return masks


def gather_blocks(x):
    for mask in doublings(lax.axis_size("exp")):
        x = jnp.concatenate([x, swap(x, "exp", mask)], axis=0)
    return x


def block_offsets(size):
    offsets = [0]
    for mask in doublings(size):
        offsets = offsets + [o ^ mask for o in offsets]
    return offsets


def scatter_sum(x):
    for mask in reversed(doublings(lax.axis_size("exp"))):
        half = x.shape[0] // 2
        x = x[:half] + swap(x[half:].astype(jnp.bfloat16), "exp", mask).astype(jnp.float32)
    return x


def sum_feat(x):
    for mask in doublings(lax.axis_size("feat")):
        x = x + swap(x.astype(jnp.bfloat16), "feat", mask).astype(jnp.float32)
    return x


def rows_kernel(ids_ref, pick_ref, dec_ref, out_ref, held, sems):
    count = ids_ref.shape[0]

    def copy(j):
        start = pl.multiple_of(ids_ref[j] // GROUP * GROUP, GROUP)
        return pltpu.make_async_copy(
            dec_ref.at[pl.ds(start, GROUP)], held.at[pl.ds(j * GROUP, GROUP)], sems.at[j]
        )

    for j in range(count):
        copy(j).start()
    for j in range(count):
        copy(j).wait()
    out_ref[...] = jnp.dot(pick_ref[...], held[...], preferred_element_type=jnp.float32).astype(
        out_ref.dtype
    )


def decoder_rows(dec_weight, safe_ids, inside):
    count, width = safe_ids.shape[0], dec_weight.shape[1]
    column = jnp.arange(count * GROUP, dtype=jnp.int32)
    wanted = jnp.arange(count, dtype=jnp.int32) * GROUP + safe_ids % GROUP
    pick = ((wanted[:, None] == column[None, :]) & inside[:, None]).astype(jnp.bfloat16)
    return pl.pallas_call(
        rows_kernel,
        out_shape=jax.ShapeDtypeStruct((count, width), jnp.bfloat16),
        in_specs=[
            pl.BlockSpec(memory_space=pltpu.SMEM),
            pl.BlockSpec(memory_space=pltpu.VMEM),
            pl.BlockSpec(memory_space=pl.ANY),
        ],
        out_specs=pl.BlockSpec(memory_space=pltpu.VMEM),
        scratch_shapes=[
            pltpu.VMEM((count * GROUP, width), jnp.bfloat16),
            pltpu.SemaphoreType.DMA((count,)),
        ],
        compiler_params=pltpu.CompilerParams(vmem_limit_bytes=24 * 1024 * 1024),
        cost_estimate=pl.CostEstimate(
            flops=2 * count * count * GROUP * width,
            bytes_accessed=2 * count * GROUP * width,
            transcendentals=0,
        ),
    )(safe_ids, pick, dec_weight)


def local_codes(route_ids, slot_limit, expert_count):
    flat_ids = route_ids.reshape(-1)
    experts = jnp.arange(expert_count, dtype=jnp.int32)
    onehot = (flat_ids[:, None] == experts[None, :]).astype(jnp.int32)
    before = jnp.sum(jnp.cumsum(onehot, axis=0) * onehot, axis=1) - 1
    slot_code = jnp.where(before < slot_limit, flat_ids * slot_limit + before, -1)
    return slot_code.reshape(route_ids.shape)


def local(
    tokens,
    route_ids,
    route_weights,
    gate_proj,
    up_proj,
    down_proj,
    enc_weight,
    enc_bias,
    dec_weight,
    dec_bias,
    clamp_ids,
    clamp_values,
):
    expert_count = lax.axis_size("exp")
    me = lax.axis_index("exp")
    row_count, width = tokens.shape
    top = route_ids.shape[1]
    half_rows = row_count // HALVES
    capacity = expert_count * SLOT
    feature_count = enc_weight.shape[1]
    offsets = jnp.array(block_offsets(expert_count), dtype=jnp.int32)

    ids_columns = jnp.pad(route_ids.astype(jnp.bfloat16), ((0, 0), (0, LANES - top)))
    outgoing = jnp.concatenate([tokens, ids_columns], axis=1)
    gathered = [
        gather_blocks(outgoing[h * half_rows : (h + 1) * half_rows]) for h in range(HALVES)
    ]
    all_tokens = [g[:, :width] for g in gathered]

    local_ids = clamp_ids - me * feature_count
    inside = (local_ids >= 0) & (local_ids < feature_count)
    safe_ids = jnp.clip(local_ids, 0, feature_count - 1)
    rows_dec = lax.psum(decoder_rows(dec_weight, safe_ids, inside), "exp")
    features = jnp.arange(feature_count, dtype=jnp.int32)
    clamp_count = clamp_ids.shape[0]
    clamp_pick = (features[:, None] == local_ids[None, :]).astype(jnp.bfloat16)
    clamp_pick = jnp.pad(clamp_pick, ((0, 0), (0, -clamp_count % LANES)))

    ids = jnp.concatenate(
        [g[:, width : width + top].reshape(expert_count, half_rows, top) for g in gathered], axis=1
    ).astype(jnp.int32)
    hit = jnp.any(ids == me, axis=2)
    order = jnp.arange(row_count)
    earlier = order[None, :] < order[:, None]
    slot = jnp.sum((hit[:, None, :] & earlier[None]).astype(jnp.int32), axis=2)
    code = jnp.where(hit & (slot < SLOT), (me ^ offsets)[:, None] * SLOT + slot, -1)
    targets = jnp.arange(capacity, dtype=jnp.int32)
    expert_in = 0.0
    for h in range(HALVES):
        part = code[:, h * half_rows : (h + 1) * half_rows].reshape(-1)
        picker = (part[None, :] == targets[:, None]).astype(jnp.bfloat16)
        expert_in += jnp.dot(picker, all_tokens[h], preferred_element_type=jnp.float32)
    expert_in = expert_in.astype(jnp.bfloat16)

    step = feature_count // CHUNKS

    def activations(h):
        acts = []
        for c in range(CHUNKS):
            part = jnp.dot(
                all_tokens[h],
                enc_weight[:, c * step : (c + 1) * step],
                preferred_element_type=jnp.float32,
            )
            pre = sum_feat(part) + enc_bias[c * step : (c + 1) * step]
            acts.append(jax.nn.relu(pre).astype(jnp.bfloat16))
        return acts

    def rebuild(acts):
        each = CHUNKS // PIECES
        rebuilt, chosen = 0.0, 0.0
        for p in range(PIECES):
            act = jnp.concatenate(acts[p * each : (p + 1) * each], axis=1)
            span = slice(p * each * step, (p + 1) * each * step)
            rebuilt += jnp.dot(act, dec_weight[span], preferred_element_type=jnp.float32)
            chosen += jnp.dot(act, clamp_pick[span], preferred_element_type=jnp.float32)
        return scatter_sum(jnp.concatenate([rebuilt, chosen], axis=1))

    acts = [activations(0)]

    gate_part = jnp.dot(expert_in, gate_proj[0], preferred_element_type=jnp.float32)
    up_part = jnp.dot(expert_in, up_proj[0], preferred_element_type=jnp.float32)
    both = sum_feat(jnp.concatenate([gate_part, up_part], axis=1))
    hidden_width = gate_part.shape[1]
    hidden = (jax.nn.silu(both[:, :hidden_width]) * both[:, hidden_width:]).astype(jnp.bfloat16)
    expert_out = jnp.dot(hidden, down_proj[0], preferred_element_type=jnp.float32).astype(
        jnp.bfloat16
    )
    returned = lax.all_to_all(
        expert_out.reshape(expert_count, SLOT, width),
        "exp",
        split_axis=0,
        concat_axis=0,
        tiled=True,
    )
    slot_code = local_codes(route_ids, SLOT, expert_count)
    matches = slot_code[None, :, :] == targets[:, None, None]
    weighted = jnp.sum(jnp.where(matches, route_weights[None, :, :], 0.0), axis=2)
    returned_rows = returned.reshape(capacity, width).astype(jnp.float32)
    moe_out = jnp.einsum("cr,cd->rd", weighted, returned_rows, precision=lax.Precision.HIGHEST)

    for h in range(1, HALVES):
        acts.append(activations(h))
    summed = jnp.concatenate([rebuild(a) for a in acts], axis=0)
    chosen = summed[:, width : width + clamp_count]
    change = clamp_values.astype(jnp.float32)[None, :] - chosen
    shift = jnp.dot(change, rows_dec.astype(jnp.float32), precision=lax.Precision.HIGHEST)
    error_term = moe_out - summed[:, :width] - dec_bias
    steered = moe_out + shift
    return (error_term, steered)


def solution(mesh):
    placed = (
        P("exp", "feat"),
        P("exp", None),
        P("exp", None),
        P("exp", "feat", None),
        P("exp", "feat", None),
        P("exp", None, "feat"),
        P("feat", "exp"),
        P("exp"),
        P("exp", "feat"),
        P("feat"),
        P(),
        P(),
    )
    return jax.shard_map(
        local,
        mesh=mesh,
        in_specs=placed,
        out_specs=(P("exp", "feat"), P("exp", "feat")),
        check_vma=False,
    )
```

```python
import functools

import jax
import jax.numpy as jnp
from jax import lax
from jax.experimental import pallas as pl
from jax.experimental.pallas import tpu as pltpu
from jax.sharding import PartitionSpec as P

SLOT = 8
SPLIT = (8, 8)
CUTS = ((0, 2, 4), (0, 2, 4))
LANES = 128
GROUP = 16
VMEM_LIMIT = 40 * 1024 * 1024


def swap(x, axis, mask):
    size = lax.axis_size(axis)
    return lax.ppermute(x, axis, [(i, i ^ mask) for i in range(size)])


def doublings(size):
    masks = []
    while size > 1:
        size //= 2
        masks.append(size)
    return masks


def gather_blocks(x):
    for mask in doublings(lax.axis_size("exp")):
        x = jnp.concatenate([x, swap(x, "exp", mask)], axis=0)
    return x


def block_offsets(size):
    offsets = [0]
    for mask in doublings(size):
        offsets = offsets + [o ^ mask for o in offsets]
    return offsets


def scatter_sum(keep, send):
    masks = doublings(lax.axis_size("exp"))[::-1]
    for mask in masks[:-1]:
        x = keep + swap(send, "exp", mask).astype(jnp.float32)
        half = x.shape[0] // 2
        keep, send = x[:half], x[half:].astype(jnp.bfloat16)
    return keep + swap(send, "exp", masks[-1]).astype(jnp.float32)


def share_all(x):
    for mask in doublings(lax.axis_size("exp"))[::-1]:
        x = x + swap(x, "exp", mask)
    return x


def exchange(own, send):
    masks = doublings(lax.axis_size("feat"))
    for mask in masks[:-1]:
        own = own + swap(send, "feat", mask).astype(jnp.float32)
        send = own.astype(jnp.bfloat16)
    return own, swap(send, "feat", masks[-1])


def tile_of(size):
    return 256 if size % 256 == 0 else LANES


def whole():
    return pl.BlockSpec(memory_space=pltpu.VMEM)


def untouched():
    return pl.BlockSpec(memory_space=pl.ANY)


def encode_kernel(tile, tokens_ref, weight_ref, *refs):
    own_ref, send_ref = refs[-2:]
    depth = weight_ref.shape[0]
    part = jnp.dot(tokens_ref[:, :depth], weight_ref[...], preferred_element_type=jnp.float32)
    columns = pl.ds(pl.multiple_of(pl.program_id(0) * tile, tile), tile)
    own_ref[:, columns] = part
    send_ref[:, columns] = part.astype(send_ref.dtype)


def encode(rows, weight, first, last, after):
    depth, count = weight.shape[0], last - first
    tile = tile_of(count)
    base = first // tile
    return pl.pallas_call(
        functools.partial(encode_kernel, tile),
        grid=(count // tile,),
        out_shape=[
            jax.ShapeDtypeStruct((rows.shape[0], count), jnp.float32),
            jax.ShapeDtypeStruct((rows.shape[0], count), jnp.bfloat16),
        ],
        in_specs=[whole(), pl.BlockSpec((depth, tile), lambda j: (0, base + j))]
        + [untouched()] * len(after),
        out_specs=[whole(), whole()],
        compiler_params=pltpu.CompilerParams(vmem_limit_bytes=VMEM_LIMIT),
        cost_estimate=pl.CostEstimate(
            flops=rows.shape[0] * depth * count // 4,
            bytes_accessed=depth * count // 4,
            transcendentals=0,
        ),
    )(rows, weight, *after)


def decode_kernel(tile, tiles, first, last, own_ref, recv_ref, bias_ref, pick_ref, weight_ref, *refs):
    act = refs[-1]
    step = pl.program_id(0)
    width = tile * tiles

    @pl.when(step == 0)
    def _():
        pre = own_ref[...] + recv_ref[...].astype(jnp.float32) + bias_ref[...]
        act[...] = jnp.maximum(pre, 0.0).astype(act.dtype)

    def put(part, columns):
        if not first:
            part = part + refs[0][:, columns]
        if last:
            keep_ref, send_ref = refs[-3:-1]
            half = part.shape[0] // 2
            keep_ref[:, columns] = part[:half]
            send_ref[:, columns] = part[half:].astype(send_ref.dtype)
        else:
            refs[-2][:, columns] = part

    @pl.when(step < tiles)
    def _():
        put(
            jnp.dot(act[...], weight_ref[...], preferred_element_type=jnp.float32),
            pl.ds(pl.multiple_of(step * tile, tile), tile),
        )

    @pl.when(step == tiles)
    def _():
        put(
            jnp.dot(act[...], pick_ref[...], preferred_element_type=jnp.float32),
            slice(width, width + LANES),
        )


def decode(own, recv, bias, pick, weight, start, total, last, after):
    rows, count = own.shape
    width = weight.shape[1]
    tile = tile_of(width)
    tiles = width // tile
    block = start // count
    first = total is None
    if last:
        out_shape = [
            jax.ShapeDtypeStruct((rows // 2, width + LANES), jnp.float32),
            jax.ShapeDtypeStruct((rows // 2, width + LANES), jnp.float32),
        ]
    else:
        out_shape = [jax.ShapeDtypeStruct((rows, width + LANES), jnp.float32)]
    operands = [own, recv, bias[start : start + count].reshape(1, count), pick[start : start + count], weight]
    in_specs = [whole()] * 4 + [
        pl.BlockSpec((count, tile), lambda j: (block, jnp.minimum(j, tiles - 1)))
    ]
    if not first:
        operands.append(total)
        in_specs.append(whole())
    out = pl.pallas_call(
        functools.partial(decode_kernel, tile, tiles, first, last),
        grid=(tiles + 1,),
        out_shape=out_shape,
        in_specs=in_specs + [untouched()] * len(after),
        out_specs=[whole()] * len(out_shape),
        scratch_shapes=[pltpu.VMEM((rows, count), jnp.bfloat16)],
        compiler_params=pltpu.CompilerParams(vmem_limit_bytes=VMEM_LIMIT),
        cost_estimate=pl.CostEstimate(
            flops=rows * width * count // 4,
            bytes_accessed=width * count // 4,
            transcendentals=0,
        ),
    )(*operands, *after)
    return out if last else out[0]


def rows_kernel(ids_ref, pick_ref, dec_ref, *refs):
    out_ref, held, sems = refs[-3:]
    count = ids_ref.shape[0]

    def copy(j):
        start = pl.multiple_of(ids_ref[j] // GROUP * GROUP, GROUP)
        return pltpu.make_async_copy(
            dec_ref.at[pl.ds(start, GROUP)], held.at[pl.ds(j * GROUP, GROUP)], sems.at[j]
        )

    for j in range(count):
        copy(j).start()
    for j in range(count):
        copy(j).wait()
    out_ref[...] = jnp.dot(pick_ref[...], held[...], preferred_element_type=jnp.float32).astype(
        out_ref.dtype
    )


def decoder_rows(dec_weight, safe_ids, inside, after):
    count, width = safe_ids.shape[0], dec_weight.shape[1]
    column = jnp.arange(count * GROUP, dtype=jnp.int32)
    wanted = jnp.arange(count, dtype=jnp.int32) * GROUP + safe_ids % GROUP
    pick = ((wanted[:, None] == column[None, :]) & inside[:, None]).astype(jnp.bfloat16)
    return pl.pallas_call(
        rows_kernel,
        out_shape=jax.ShapeDtypeStruct((count, width), jnp.bfloat16),
        in_specs=[
            pl.BlockSpec(memory_space=pltpu.SMEM),
            whole(),
            pl.BlockSpec(memory_space=pltpu.HBM),
        ]
        + [untouched()] * len(after),
        out_specs=whole(),
        scratch_shapes=[
            pltpu.VMEM((count * GROUP, width), jnp.bfloat16),
            pltpu.SemaphoreType.DMA((count,)),
        ],
        compiler_params=pltpu.CompilerParams(vmem_limit_bytes=VMEM_LIMIT),
        cost_estimate=pl.CostEstimate(
            flops=count * count * GROUP * width,
            bytes_accessed=count * GROUP * width,
            transcendentals=0,
        ),
    )(safe_ids, pick, dec_weight, *after)


def local_codes(route_ids, slot_limit, expert_count):
    flat_ids = route_ids.reshape(-1)
    experts = jnp.arange(expert_count, dtype=jnp.int32)
    onehot = (flat_ids[:, None] == experts[None, :]).astype(jnp.int32)
    before = jnp.sum(jnp.cumsum(onehot, axis=0) * onehot, axis=1) - 1
    slot_code = jnp.where(before < slot_limit, flat_ids * slot_limit + before, -1)
    return slot_code.reshape(route_ids.shape)


def local(
    tokens,
    route_ids,
    route_weights,
    gate_proj,
    up_proj,
    down_proj,
    enc_weight,
    enc_bias,
    dec_weight,
    dec_bias,
    clamp_ids,
    clamp_values,
):
    expert_count = lax.axis_size("exp")
    me = lax.axis_index("exp")
    row_count, width = tokens.shape
    top = route_ids.shape[1]
    capacity = expert_count * SLOT
    feature_count = enc_weight.shape[1]
    offsets = jnp.array(block_offsets(expert_count), dtype=jnp.int32)
    edges = [0]
    for rows in SPLIT:
        edges.append(edges[-1] + rows)

    ids_columns = jnp.pad(route_ids.astype(jnp.bfloat16), ((0, 0), (0, LANES - top)))
    outgoing = jnp.concatenate([tokens, ids_columns], axis=1)
    gathered = [gather_blocks(outgoing[a:b]) for a, b in zip(edges, edges[1:])]

    cuts = [[feature_count * c // cut[-1] for c in cut] for cut in CUTS]

    own, recv, sends = {}, {}, {}

    def send_part(h, c, after):
        mine, send = encode(gathered[h], enc_weight, cuts[h][c], cuts[h][c + 1], after)
        sends[h, c] = send
        own[h, c], recv[h, c] = exchange(mine, send)

    send_part(0, 0, [])
    send_part(0, 1, [sends[0, 0]])

    ids = jnp.concatenate(
        [
            g[:, width : width + top].reshape(expert_count, rows, top)
            for g, rows in zip(gathered, SPLIT)
        ],
        axis=1,
    ).astype(jnp.int32)
    hit = jnp.any(ids == me, axis=2)
    order = jnp.arange(row_count)
    earlier = order[None, :] < order[:, None]
    slot = jnp.sum((hit[:, None, :] & earlier[None]).astype(jnp.int32), axis=2)
    code = jnp.where(hit & (slot < SLOT), (me ^ offsets)[:, None] * SLOT + slot, -1)
    targets = jnp.arange(capacity, dtype=jnp.int32)
    expert_in = 0.0
    for h, (a, b) in enumerate(zip(edges, edges[1:])):
        picker = (code[:, a:b].reshape(-1)[None, :] == targets[:, None]).astype(jnp.bfloat16)
        expert_in += jnp.dot(picker, gathered[h][:, :width], preferred_element_type=jnp.float32)
    expert_in = expert_in.astype(jnp.bfloat16)
    gate_part = jnp.dot(expert_in, gate_proj[0], preferred_element_type=jnp.float32)
    up_part = jnp.dot(expert_in, up_proj[0], preferred_element_type=jnp.float32)
    both_part = jnp.concatenate([gate_part, up_part], axis=1)
    both_send = both_part.astype(jnp.bfloat16)
    both_own, both_recv = exchange(both_part, both_send)

    send_part(1, 0, [recv[0, 0], both_send])
    send_part(1, 1, [recv[0, 1], sends[1, 0]])

    local_ids = clamp_ids - me * feature_count
    inside = (local_ids >= 0) & (local_ids < feature_count)
    safe_ids = jnp.clip(local_ids, 0, feature_count - 1)
    rows_dec = share_all(decoder_rows(dec_weight, safe_ids, inside, [sends[1, 1]]))
    features = jnp.arange(feature_count, dtype=jnp.int32)
    clamp_count = clamp_ids.shape[0]
    clamp_pick = (features[:, None] == local_ids[None, :]).astype(jnp.bfloat16)
    clamp_pick = jnp.pad(clamp_pick, ((0, 0), (0, -clamp_count % LANES)))

    def rebuild(h, after):
        total, parts = None, len(cuts[h]) - 1
        for c in range(parts):
            total = decode(
                own[h, c],
                recv[h, c],
                enc_bias,
                clamp_pick,
                dec_weight,
                cuts[h][c],
                total,
                c == parts - 1,
                after,
            )
        return scatter_sum(*total)

    summed = [rebuild(0, [sends[1, 1]])]

    both = both_own + both_recv.astype(jnp.float32)
    hidden_width = gate_part.shape[1]
    hidden = (jax.nn.silu(both[:, :hidden_width]) * both[:, hidden_width:]).astype(jnp.bfloat16)
    expert_out = jnp.dot(hidden, down_proj[0], preferred_element_type=jnp.float32).astype(
        jnp.bfloat16
    )
    returned = lax.all_to_all(
        expert_out.reshape(expert_count, SLOT, width),
        "exp",
        split_axis=0,
        concat_axis=0,
        tiled=True,
    )
    slot_code = local_codes(route_ids, SLOT, expert_count)
    matches = slot_code[None, :, :] == targets[:, None, None]
    weighted = jnp.sum(jnp.where(matches, route_weights[None, :, :], 0.0), axis=2)
    returned_rows = returned.reshape(capacity, width).astype(jnp.float32)
    moe_out = jnp.einsum("cr,cd->rd", weighted, returned_rows, precision=lax.Precision.HIGHEST)

    summed.append(rebuild(1, [expert_out]))
    summed = jnp.concatenate(summed, axis=0)
    chosen = summed[:, width : width + clamp_count]
    change = clamp_values.astype(jnp.float32)[None, :] - chosen
    shift = jnp.dot(change, rows_dec.astype(jnp.float32), precision=lax.Precision.HIGHEST)
    error_term = moe_out - summed[:, :width] - dec_bias
    steered = moe_out + shift
    return (error_term, steered)


def solution(mesh):
    placed = (
        P("exp", "feat"),
        P("exp", None),
        P("exp", None),
        P("exp", "feat", None),
        P("exp", "feat", None),
        P("exp", None, "feat"),
        P("feat", "exp"),
        P("exp"),
        P("exp", "feat"),
        P("feat"),
        P(),
        P(),
    )
    return jax.shard_map(
        local,
        mesh=mesh,
        in_specs=placed,
        out_specs=(P("exp", "feat"), P("exp", "feat")),
        check_vma=False,
    )
```

```python
import functools

import jax
import jax.numpy as jnp
from jax import lax
from jax.experimental import pallas as pl
from jax.experimental.pallas import tpu as pltpu
from jax.sharding import PartitionSpec as P

SLOT = 8
SPLIT = (8, 8)
CUTS = ((0, 2, 4), (0, 2, 4))
LANES = 128
FRACTION = 2
VMEM_LIMIT = 36 * 1024 * 1024
ROWS_LIMIT = 56 * 1024 * 1024


def swap(x, axis, mask):
    size = lax.axis_size(axis)
    return lax.ppermute(x, axis, [(i, i ^ mask) for i in range(size)])


def doublings(size):
    masks = []
    while size > 1:
        size //= 2
        masks.append(size)
    return masks


def gather_blocks(x):
    for mask in doublings(lax.axis_size("exp")):
        x = jnp.concatenate([x, swap(x, "exp", mask)], axis=0)
    return x


def block_offsets(size):
    offsets = [0]
    for mask in doublings(size):
        offsets = offsets + [o ^ mask for o in offsets]
    return offsets


def behind(x, *others):
    return lax.optimization_barrier((x, *others))[0]


def scatter_masks():
    return doublings(lax.axis_size("exp"))[::-1]


def add_swapped(keep, send, mask, wait):
    return keep + behind(swap(send, "exp", mask), *wait).astype(jnp.float32)


def halves(x, groups):
    low, high, start = [], [], 0
    for g in groups:
        low.append(x[start : start + g])
        high.append(x[start + g : start + 2 * g])
        start += 2 * g
    keep = jnp.concatenate(low, axis=0) if len(low) > 1 else low[0]
    send = jnp.concatenate(high, axis=0) if len(high) > 1 else high[0]
    return keep, send.astype(jnp.bfloat16)


def scatter_steps(keep, send, groups, first, waits):
    masks = scatter_masks()
    groups = [g >> (first + 1) for g in groups]
    for k in range(first, len(masks) - 1):
        x = add_swapped(keep, send, masks[k], waits.get(k, ()))
        keep, send = halves(x, groups)
        groups = [g // 2 for g in groups]
    return add_swapped(keep, send, masks[-1], waits.get(len(masks) - 1, ()))


def exchange(own, send):
    masks = doublings(lax.axis_size("feat"))
    for mask in masks[:-1]:
        own = own + swap(send, "feat", mask).astype(jnp.float32)
        send = own.astype(jnp.bfloat16)
    return own, swap(send, "feat", masks[-1])


def tile_of(size):
    return next(t for t in (512, 256, LANES) if size % t == 0)


def whole():
    return pl.BlockSpec(memory_space=pltpu.VMEM)


def untouched():
    return pl.BlockSpec(memory_space=pl.ANY)


def params(limit=VMEM_LIMIT):
    return pltpu.CompilerParams(vmem_limit_bytes=limit)


def cost(flops, size):
    return pl.CostEstimate(flops=flops, bytes_accessed=size, transcendentals=0)


def stream(weight_ref, rows, first, tile, tiles, held, sems):
    def copy(j):
        columns = pl.ds(pl.multiple_of(first + j * tile, tile), tile)
        return pltpu.make_async_copy(weight_ref.at[rows, columns], held.at[j], sems.at[j])

    for j in range(tiles):
        copy(j).start()
    return copy


def encode_kernel(first, count, tokens_ref, weight_ref, *refs):
    own_ref, send_ref, held, sems = refs[-4:]
    depth = weight_ref.shape[0]
    tiles, _, tile = held.shape
    copy = stream(weight_ref, slice(0, depth), first, tile, tiles, held, sems)

    def step(j, carry):
        copy(j).wait()
        here = pl.ds(pl.multiple_of(j * tile, tile), tile)
        part = jnp.dot(tokens_ref[:, :depth], held[j], preferred_element_type=jnp.float32)
        own_ref[:, here] = part
        send_ref[:, here] = part.astype(send_ref.dtype)
        return carry

    lax.fori_loop(0, tiles, step, 0)


def encode(rows, weight, first, last, after):
    depth, count = weight.shape[0], last - first
    tile = tile_of(count)
    tiles = count // tile
    return pl.pallas_call(
        functools.partial(encode_kernel, first, count),
        out_shape=[
            jax.ShapeDtypeStruct((rows.shape[0], count), jnp.float32),
            jax.ShapeDtypeStruct((rows.shape[0], count), jnp.bfloat16),
        ],
        in_specs=[whole(), pl.BlockSpec(memory_space=pltpu.HBM)] + [untouched()] * len(after),
        out_specs=[whole(), whole()],
        scratch_shapes=[
            pltpu.VMEM((tiles, depth, tile), weight.dtype),
            pltpu.SemaphoreType.DMA((tiles,)),
        ],
        compiler_params=params(),
        cost_estimate=cost(rows.shape[0] * depth * count // FRACTION, depth * count // FRACTION),
    )(rows, weight, *after)


def expert_kernel(pick0_ref, pick1_ref, rows0_ref, rows1_ref, gate_ref, up_ref, *refs):
    own_ref, send_ref, rows, held, sems = refs[-5:]
    _, depth, width = gate_ref.shape
    tiles, _, tile = held.shape
    each = tiles // 2

    def copy(ref, j, slot):
        columns = slice(j * tile, (j + 1) * tile)
        return pltpu.make_async_copy(ref.at[0, :, columns], held.at[slot], sems.at[slot])

    copies = [copy(gate_ref, j, j) for j in range(each)]
    copies += [copy(up_ref, j, each + j) for j in range(each)]
    for c in copies:
        c.start()
    for first in range(0, depth, 512):
        last = min(first + 512, depth)
        part = jnp.dot(
            pick0_ref[...], rows0_ref[:, first:last], preferred_element_type=jnp.float32
        )
        part += jnp.dot(
            pick1_ref[...], rows1_ref[:, first:last], preferred_element_type=jnp.float32
        )
        rows[:, first:last] = part.astype(rows.dtype)
    for j in range(tiles):
        copies[j].wait()
        part = jnp.dot(rows[...], held[j], preferred_element_type=jnp.float32)
        own_ref[:, j * tile : (j + 1) * tile] = part
        send_ref[:, j * tile : (j + 1) * tile] = part.astype(send_ref.dtype)


def expert_halves(picks, rows, gate, up, after):
    capacity, depth, width = picks[0].shape[0], gate.shape[1], gate.shape[2]
    tile = tile_of(width)
    tiles = 2 * (width // tile)
    hbm = pl.BlockSpec(memory_space=pltpu.HBM)
    return pl.pallas_call(
        expert_kernel,
        out_shape=[
            jax.ShapeDtypeStruct((capacity, 2 * width), jnp.float32),
            jax.ShapeDtypeStruct((capacity, 2 * width), jnp.bfloat16),
        ],
        in_specs=[whole()] * 4 + [hbm, hbm] + [untouched()] * len(after),
        out_specs=[whole(), whole()],
        scratch_shapes=[
            pltpu.VMEM((capacity, depth), jnp.bfloat16),
            pltpu.VMEM((tiles, depth, tile), gate.dtype),
            pltpu.SemaphoreType.DMA((tiles,)),
        ],
        compiler_params=params(ROWS_LIMIT),
        cost_estimate=cost(2 * capacity * depth * width // FRACTION, 2 * depth * width // FRACTION),
    )(*picks, *rows, gate, up, *after)


def decode_kernel(start, first, last, own_ref, recv_ref, bias_ref, pick_ref, want_ref, weight_ref, *refs):
    act, held, sems = refs[-3:]
    refs = refs[:-2]
    count, width = own_ref.shape[1], weight_ref.shape[1]
    tiles, _, tile = held.shape
    copy = stream(weight_ref, slice(start, start + count), 0, tile, tiles, held, sems)
    pre = own_ref[...] + recv_ref[...].astype(jnp.float32) + bias_ref[...]
    rows, extra = own_ref.shape[0], act.shape[0] - own_ref.shape[0]
    act[:rows] = jnp.maximum(pre, 0.0).astype(act.dtype)
    if extra:
        act[rows:] = want_ref[...]

    def put(part, columns):
        if not first:
            part = part + refs[0][:, columns]
        if last:
            start = 0
            for ref in refs[-3:-1]:
                ref[: rows // 2, columns] = part[start * rows // 2 : (start + 1) * rows // 2]
                if extra:
                    at = rows + start * extra // 2
                    ref[rows // 2 :, columns] = part[at : at + extra // 2]
                start += 1
        else:
            refs[-2][:, columns] = part

    def step(j, carry):
        columns = pl.ds(pl.multiple_of(j * tile, tile), tile)
        copy(j).wait()
        put(jnp.dot(act[...], held[j], preferred_element_type=jnp.float32), columns)
        return carry

    lax.fori_loop(0, tiles, step, 0)
    put(
        jnp.dot(act[...], pick_ref[...], preferred_element_type=jnp.float32),
        slice(width, width + LANES),
    )


def decode(own, recv, bias, pick, want, weight, start, total, last, after):
    rows, count = own.shape
    width = weight.shape[1]
    extra = 0 if want is None else want.shape[0]
    tile = tile_of(width)
    tiles = width // tile
    first = total is None
    if last:
        out_shape = [
            jax.ShapeDtypeStruct(((rows + extra) // 2, width + LANES), jnp.float32)
        ] * 2
    else:
        out_shape = [jax.ShapeDtypeStruct((rows + extra, width + LANES), jnp.float32)]
    operands = [
        own,
        recv,
        bias[start : start + count].reshape(1, count),
        pick[start : start + count],
        pick[:8, :8] if want is None else want[:, start : start + count],
        weight,
    ]
    in_specs = [whole()] * 5 + [pl.BlockSpec(memory_space=pltpu.HBM)]
    if not first:
        operands.append(total)
        in_specs.append(whole())
    out = pl.pallas_call(
        functools.partial(decode_kernel, start, first, last),
        out_shape=out_shape,
        in_specs=in_specs + [untouched()] * len(after),
        out_specs=[whole()] * len(out_shape),
        scratch_shapes=[
            pltpu.VMEM((rows + extra, count), jnp.bfloat16),
            pltpu.VMEM((tiles, count, tile), weight.dtype),
            pltpu.SemaphoreType.DMA((tiles,)),
        ],
        compiler_params=params(),
        cost_estimate=cost(rows * width * count // FRACTION, width * count // FRACTION),
    )(*operands, *after)
    return out if last else out[0]


def local(
    tokens,
    route_ids,
    route_weights,
    gate_proj,
    up_proj,
    down_proj,
    enc_weight,
    enc_bias,
    dec_weight,
    dec_bias,
    clamp_ids,
    clamp_values,
):
    expert_count = lax.axis_size("exp")
    me = lax.axis_index("exp")
    row_count, width = tokens.shape
    top = route_ids.shape[1]
    capacity = expert_count * SLOT
    feature_count = enc_weight.shape[1]
    edges = [0]
    for rows in SPLIT:
        edges.append(edges[-1] + rows)

    weights_high = route_weights.astype(jnp.bfloat16)
    weights_low = (route_weights - weights_high.astype(jnp.float32)).astype(jnp.bfloat16)
    routing = jnp.concatenate(
        [route_ids.astype(jnp.bfloat16), weights_high, weights_low], axis=1
    )
    outgoing = jnp.concatenate(
        [tokens, jnp.pad(routing, ((0, 0), (0, LANES - 3 * top)))], axis=1
    )
    gathered = [gather_blocks(outgoing[a:b]) for a, b in zip(edges, edges[1:])]

    local_ids = clamp_ids - me * feature_count
    offsets = jnp.array(block_offsets(expert_count), dtype=jnp.int32)
    clamp_count = clamp_ids.shape[0]
    each = clamp_count // expert_count
    turn = (me ^ offsets)[:, None] * each + jnp.arange(each, dtype=jnp.int32)[None, :]
    turn = turn.reshape(-1)[:, None] == jnp.arange(clamp_count, dtype=jnp.int32)[None, :]
    turned_ids = jnp.sum(jnp.where(turn, local_ids[None, :], 0), axis=1)
    features = jnp.arange(feature_count, dtype=jnp.int32)
    clamp_pick = (features[:, None] == local_ids[None, :]).astype(jnp.bfloat16)
    clamp_pick = jnp.pad(clamp_pick, ((0, 0), (0, -clamp_count % LANES)))
    clamp_want = (features[None, :] == turned_ids[:, None]).astype(jnp.bfloat16)

    cuts = [[feature_count * c // cut[-1] for c in cut] for cut in CUTS]
    own, recv, sends = {}, {}, {}

    def send_part(h, c, after):
        mine, send = encode(gathered[h], enc_weight, cuts[h][c], cuts[h][c + 1], after)
        sends[h, c] = send
        own[h, c], recv[h, c] = exchange(mine, send)

    send_part(0, 0, [])

    routed = jnp.concatenate(
        [
            g[:, width:].reshape(expert_count, rows, LANES)
            for g, rows in zip(gathered, SPLIT)
        ],
        axis=1,
    ).astype(jnp.float32)
    named = routed[:, :, :top].astype(jnp.int32) == me
    share = routed[:, :, top : 2 * top] + routed[:, :, 2 * top : 3 * top]
    share = jnp.sum(jnp.where(named, share, 0.0), axis=2)
    hit = jnp.any(named, axis=2)
    order = jnp.arange(row_count)
    earlier = order[None, :] < order[:, None]
    slot = jnp.sum((hit[:, None, :] & earlier[None]).astype(jnp.int32), axis=2)
    place = jnp.arange(expert_count, dtype=jnp.int32)[:, None] * SLOT + slot
    code = jnp.where(hit & (slot < SLOT), place, -1)
    targets = jnp.arange(capacity, dtype=jnp.int32)
    picks = [
        (code[:, a:b].reshape(-1)[None, :] == targets[:, None]).astype(jnp.bfloat16)
        for a, b in zip(edges, edges[1:])
    ]
    both_part, both_send = expert_halves(
        picks, gathered, gate_proj, up_proj, [sends[0, 0]]
    )
    both_own, both_recv = exchange(both_part, both_send)

    send_part(0, 1, [both_send])
    send_part(1, 0, [sends[0, 1], recv[0, 0]])

    both = both_own + behind(both_recv, sends[1, 0]).astype(jnp.float32)
    hidden_width = gate_proj.shape[2]
    hidden = (jax.nn.silu(both[:, :hidden_width]) * both[:, hidden_width:]).astype(jnp.bfloat16)
    expert_out = jnp.dot(hidden, down_proj[0], preferred_element_type=jnp.float32).astype(
        jnp.bfloat16
    )

    def returned(a, b):
        picker = (code[a:b].reshape(-1)[:, None] == targets[None, :]).astype(jnp.bfloat16)
        rows = jnp.dot(picker, expert_out, preferred_element_type=jnp.float32)
        return rows * share[a:b].reshape(-1)[:, None]

    send_part(1, 1, [sends[1, 0], recv[0, 1]])

    half = expert_count // 2
    moe_send = returned(half, expert_count).astype(jnp.bfloat16)

    moe_rows = moe_send.shape[0]
    mask = scatter_masks()[0]
    moe_keep, moe_next = halves(
        add_swapped(returned(0, half), moe_send, mask, [recv[1, 0]]), [moe_rows // 2]
    )

    def rebuild(h, c, total, want, after):
        start, last = cuts[h][c], c == len(cuts[h]) - 2
        return decode(
            own[h, c], recv[h, c], enc_bias, clamp_pick, want, dec_weight, start, total, last, after
        )

    part = rebuild(0, 0, None, clamp_want, [sends[1, 1]])
    keep, send = rebuild(0, 1, part, clamp_want, [recv[1, 0]])
    part = rebuild(1, 0, None, None, [send, moe_next])
    groups = [keep.shape[0] - clamp_count // 2, clamp_count // 2]
    first = add_swapped(keep, send, mask, [part, recv[1, 1]])
    first_keep, first_next = halves(first, [g // 2 for g in groups])
    last_keep, last_send = rebuild(1, 1, part, None, [first_next, moe_next])
    second_keep, second_next = halves(
        add_swapped(last_keep, last_send, mask, []), [last_keep.shape[0] // 2]
    )
    moe_out = scatter_steps(moe_keep, moe_next, [moe_rows], 1, {1: [second_next]})
    first = scatter_steps(first_keep, first_next, groups, 1, {1: [second_next]})
    rows_dec = gather_blocks(first[SPLIT[0] :, :width].astype(jnp.bfloat16))
    second = scatter_steps(second_keep, second_next, [last_keep.shape[0]], 1, {})
    summed = jnp.concatenate([first[: SPLIT[0]], second], axis=0)
    chosen = summed[:, width : width + clamp_count]
    change = clamp_values.astype(jnp.float32)[None, :] - chosen
    change = jnp.dot(change, turn.T.astype(jnp.float32), precision=lax.Precision.HIGHEST)
    shift = jnp.dot(change, rows_dec.astype(jnp.float32), precision=lax.Precision.HIGHEST)
    error_term = moe_out - summed[:, :width] - dec_bias
    steered = moe_out + shift
    return (error_term, steered)


def solution(mesh):
    placed = (
        P("exp", "feat"),
        P("exp", None),
        P("exp", None),
        P("exp", "feat", None),
        P("exp", "feat", None),
        P("exp", None, "feat"),
        P("feat", "exp"),
        P("exp"),
        P("exp", "feat"),
        P("feat"),
        P(),
        P(),
    )
    return jax.shard_map(
        local,
        mesh=mesh,
        in_specs=placed,
        out_specs=(P("exp", "feat"), P("exp", "feat")),
        check_vma=False,
    )
```

```python
import functools

import jax
import jax.numpy as jnp
from jax import lax
from jax.experimental import pallas as pl
from jax.experimental.pallas import tpu as pltpu
from jax.sharding import PartitionSpec as P

SLOT = 8
SPLIT = (8, 8)
CUTS = ((0, 2, 8), (0, 5, 8))
LANES = 128
LASTS = (0, 1)
FRACTION = 2
VMEM_LIMIT = 36 * 1024 * 1024
ROWS_LIMIT = 56 * 1024 * 1024


def swap(x, axis, mask):
    size = lax.axis_size(axis)
    return lax.ppermute(x, axis, [(i, i ^ mask) for i in range(size)])


def doublings(size):
    masks = []
    while size > 1:
        size //= 2
        masks.append(size)
    return masks


def gather_blocks(x):
    for mask in doublings(lax.axis_size("exp")):
        x = jnp.concatenate([x, swap(x, "exp", mask)], axis=0)
    return x


def block_offsets(size):
    offsets = [0]
    for mask in doublings(size):
        offsets = offsets + [o ^ mask for o in offsets]
    return offsets


def behind(x, *others):
    return lax.optimization_barrier((x, *others))[0]


def scatter_masks():
    return doublings(lax.axis_size("exp"))[::-1]


def add_swapped(keep, send, mask, wait):
    return keep + behind(swap(send, "exp", mask), *wait).astype(jnp.float32)


def halves(x, groups):
    low, high, start = [], [], 0
    for g in groups:
        low.append(x[start : start + g])
        high.append(x[start + g : start + 2 * g])
        start += 2 * g
    keep = jnp.concatenate(low, axis=0) if len(low) > 1 else low[0]
    send = jnp.concatenate(high, axis=0) if len(high) > 1 else high[0]
    return keep, send.astype(jnp.bfloat16)


def scatter_steps(keep, send, groups, first, waits):
    masks = scatter_masks()
    groups = [g >> (first + 1) for g in groups]
    for k in range(first, len(masks) - 1):
        x = add_swapped(keep, send, masks[k], waits.get(k, ()))
        keep, send = halves(x, groups)
        groups = [g // 2 for g in groups]
    return add_swapped(keep, send, masks[-1], waits.get(len(masks) - 1, ()))


def exchange(own, send):
    masks = doublings(lax.axis_size("feat"))
    for mask in masks[:-1]:
        own = own + swap(send, "feat", mask).astype(jnp.float32)
        send = own.astype(jnp.bfloat16)
    return own, swap(send, "feat", masks[-1])


def tile_of(size):
    return next(t for t in (512, 256, LANES) if size % t == 0)


def whole():
    return pl.BlockSpec(memory_space=pltpu.VMEM)


def untouched():
    return pl.BlockSpec(memory_space=pl.ANY)


def params(limit=VMEM_LIMIT):
    return pltpu.CompilerParams(vmem_limit_bytes=limit)


def cost(flops, size):
    return pl.CostEstimate(flops=flops, bytes_accessed=size, transcendentals=0)


def stream(weight_ref, rows, first, tile, tiles, held, sems):
    def copy(j):
        columns = pl.ds(pl.multiple_of(first + j * tile, tile), tile)
        return pltpu.make_async_copy(weight_ref.at[rows, columns], held.at[j], sems.at[j])

    for j in range(tiles):
        copy(j).start()
    return copy


def encode_kernel(first, count, tokens_ref, weight_ref, *refs):
    own_ref, send_ref, held, sems = refs[-4:]
    depth = weight_ref.shape[0]
    tiles, _, tile = held.shape
    copy = stream(weight_ref, slice(0, depth), first, tile, tiles, held, sems)

    def step(j, carry):
        copy(j).wait()
        here = pl.ds(pl.multiple_of(j * tile, tile), tile)
        part = jnp.dot(tokens_ref[:, :depth], held[j], preferred_element_type=jnp.float32)
        own_ref[:, here] = part
        send_ref[:, here] = part.astype(send_ref.dtype)
        return carry

    lax.fori_loop(0, tiles, step, 0)


def encode(rows, weight, first, last, after):
    depth, count = weight.shape[0], last - first
    tile = tile_of(count)
    tiles = count // tile
    return pl.pallas_call(
        functools.partial(encode_kernel, first, count),
        out_shape=[
            jax.ShapeDtypeStruct((rows.shape[0], count), jnp.float32),
            jax.ShapeDtypeStruct((rows.shape[0], count), jnp.bfloat16),
        ],
        in_specs=[whole(), pl.BlockSpec(memory_space=pltpu.HBM)] + [untouched()] * len(after),
        out_specs=[whole(), whole()],
        scratch_shapes=[
            pltpu.VMEM((tiles, depth, tile), weight.dtype),
            pltpu.SemaphoreType.DMA((tiles,)),
        ],
        compiler_params=params(),
        cost_estimate=cost(rows.shape[0] * depth * count // FRACTION, depth * count // FRACTION),
    )(rows, weight, *after)


def expert_kernel(pick0_ref, pick1_ref, rows0_ref, rows1_ref, gate_ref, up_ref, *refs):
    own_ref, send_ref, rows, held, sems = refs[-5:]
    _, depth, width = gate_ref.shape
    tiles, _, tile = held.shape
    each = tiles // 2

    def copy(ref, j, slot):
        columns = slice(j * tile, (j + 1) * tile)
        return pltpu.make_async_copy(ref.at[0, :, columns], held.at[slot], sems.at[slot])

    copies = [copy(gate_ref, j, j) for j in range(each)]
    copies += [copy(up_ref, j, each + j) for j in range(each)]
    for c in copies:
        c.start()
    for first in range(0, depth, 512):
        last = min(first + 512, depth)
        part = jnp.dot(
            pick0_ref[...], rows0_ref[:, first:last], preferred_element_type=jnp.float32
        )
        part += jnp.dot(
            pick1_ref[...], rows1_ref[:, first:last], preferred_element_type=jnp.float32
        )
        rows[:, first:last] = part.astype(rows.dtype)
    for j in range(tiles):
        copies[j].wait()
        part = jnp.dot(rows[...], held[j], preferred_element_type=jnp.float32)
        own_ref[:, j * tile : (j + 1) * tile] = part
        send_ref[:, j * tile : (j + 1) * tile] = part.astype(send_ref.dtype)


def expert_halves(picks, rows, gate, up, after):
    capacity, depth, width = picks[0].shape[0], gate.shape[1], gate.shape[2]
    tile = tile_of(width)
    tiles = 2 * (width // tile)
    hbm = pl.BlockSpec(memory_space=pltpu.HBM)
    return pl.pallas_call(
        expert_kernel,
        out_shape=[
            jax.ShapeDtypeStruct((capacity, 2 * width), jnp.float32),
            jax.ShapeDtypeStruct((capacity, 2 * width), jnp.bfloat16),
        ],
        in_specs=[whole()] * 4 + [hbm, hbm] + [untouched()] * len(after),
        out_specs=[whole(), whole()],
        scratch_shapes=[
            pltpu.VMEM((capacity, depth), jnp.bfloat16),
            pltpu.VMEM((tiles, depth, tile), gate.dtype),
            pltpu.SemaphoreType.DMA((tiles,)),
        ],
        compiler_params=params(ROWS_LIMIT),
        cost_estimate=cost(2 * capacity * depth * width // FRACTION, 2 * depth * width // FRACTION),
    )(*picks, *rows, gate, up, *after)


def decode_kernel(start, first, last, own_ref, recv_ref, bias_ref, pick_ref, want_ref, weight_ref, *refs):
    act, held, sems = refs[-3:]
    refs = refs[:-2]
    count, width = own_ref.shape[1], weight_ref.shape[1]
    tiles, _, tile = held.shape
    copy = stream(weight_ref, slice(start, start + count), 0, tile, tiles, held, sems)
    pre = own_ref[...] + recv_ref[...].astype(jnp.float32) + bias_ref[...]
    rows, extra = own_ref.shape[0], act.shape[0] - own_ref.shape[0]
    act[:rows] = jnp.maximum(pre, 0.0).astype(act.dtype)
    if extra:
        act[rows:] = want_ref[...]

    def put(part, columns):
        if not first:
            part = part + refs[0][:, columns]
        if last:
            start = 0
            for ref in refs[-3:-1]:
                ref[: rows // 2, columns] = part[start * rows // 2 : (start + 1) * rows // 2]
                if extra:
                    at = rows + start * extra // 2
                    ref[rows // 2 :, columns] = part[at : at + extra // 2]
                start += 1
        else:
            refs[-2][:, columns] = part

    def step(j, carry):
        columns = pl.ds(pl.multiple_of(j * tile, tile), tile)
        copy(j).wait()
        put(jnp.dot(act[...], held[j], preferred_element_type=jnp.float32), columns)
        return carry

    lax.fori_loop(0, tiles, step, 0)
    put(
        jnp.dot(act[...], pick_ref[...], preferred_element_type=jnp.float32),
        slice(width, width + LANES),
    )


def decode(own, recv, bias, pick, want, weight, start, total, last, after):
    rows, count = own.shape
    width = weight.shape[1]
    extra = 0 if want is None else want.shape[0]
    tile = tile_of(width)
    tiles = width // tile
    first = total is None
    if last:
        out_shape = [
            jax.ShapeDtypeStruct(((rows + extra) // 2, width + LANES), jnp.float32)
        ] * 2
    else:
        out_shape = [jax.ShapeDtypeStruct((rows + extra, width + LANES), jnp.float32)]
    operands = [
        own,
        recv,
        bias[start : start + count].reshape(1, count),
        pick[start : start + count],
        pick[:8, :8] if want is None else want[:, start : start + count],
        weight,
    ]
    in_specs = [whole()] * 5 + [pl.BlockSpec(memory_space=pltpu.HBM)]
    if not first:
        operands.append(total)
        in_specs.append(whole())
    out = pl.pallas_call(
        functools.partial(decode_kernel, start, first, last),
        out_shape=out_shape,
        in_specs=in_specs + [untouched()] * len(after),
        out_specs=[whole()] * len(out_shape),
        scratch_shapes=[
            pltpu.VMEM((rows + extra, count), jnp.bfloat16),
            pltpu.VMEM((tiles, count, tile), weight.dtype),
            pltpu.SemaphoreType.DMA((tiles,)),
        ],
        compiler_params=params(),
        cost_estimate=cost(rows * width * count // FRACTION, width * count // FRACTION),
    )(*operands, *after)
    return out if last else out[0]


def local(
    tokens,
    route_ids,
    route_weights,
    gate_proj,
    up_proj,
    down_proj,
    enc_weight,
    enc_bias,
    dec_weight,
    dec_bias,
    clamp_ids,
    clamp_values,
):
    expert_count = lax.axis_size("exp")
    me = lax.axis_index("exp")
    row_count, width = tokens.shape
    top = route_ids.shape[1]
    capacity = expert_count * SLOT
    feature_count = enc_weight.shape[1]
    edges = [0]
    for rows in SPLIT:
        edges.append(edges[-1] + rows)

    weights_high = route_weights.astype(jnp.bfloat16)
    weights_low = (route_weights - weights_high.astype(jnp.float32)).astype(jnp.bfloat16)
    routing = jnp.concatenate(
        [route_ids.astype(jnp.bfloat16), weights_high, weights_low], axis=1
    )
    outgoing = jnp.concatenate(
        [tokens, jnp.pad(routing, ((0, 0), (0, LANES - 3 * top)))], axis=1
    )
    gathered = [gather_blocks(outgoing[a:b]) for a, b in zip(edges, edges[1:])]

    local_ids = clamp_ids - me * feature_count
    offsets = jnp.array(block_offsets(expert_count), dtype=jnp.int32)
    clamp_count = clamp_ids.shape[0]
    each = clamp_count // expert_count
    turn = (me ^ offsets)[:, None] * each + jnp.arange(each, dtype=jnp.int32)[None, :]
    turn = turn.reshape(-1)[:, None] == jnp.arange(clamp_count, dtype=jnp.int32)[None, :]
    turned_ids = jnp.sum(jnp.where(turn, local_ids[None, :], 0), axis=1)
    features = jnp.arange(feature_count, dtype=jnp.int32)
    clamp_pick = (features[:, None] == local_ids[None, :]).astype(jnp.bfloat16)
    clamp_pick = jnp.pad(clamp_pick, ((0, 0), (0, -clamp_count % LANES)))
    clamp_want = (features[None, :] == turned_ids[:, None]).astype(jnp.bfloat16)

    cuts = [[feature_count * c // cut[-1] for c in cut] for cut in CUTS]
    own, recv, sends = {}, {}, {}

    def send_part(h, c, after):
        mine, send = encode(gathered[h], enc_weight, cuts[h][c], cuts[h][c + 1], after)
        sends[h, c] = send
        own[h, c], recv[h, c] = exchange(mine, send)

    send_part(0, 0, [])

    routed = jnp.concatenate(
        [
            g[:, width:].reshape(expert_count, rows, LANES)
            for g, rows in zip(gathered, SPLIT)
        ],
        axis=1,
    ).astype(jnp.float32)
    named = routed[:, :, :top].astype(jnp.int32) == me
    share = routed[:, :, top : 2 * top] + routed[:, :, 2 * top : 3 * top]
    share = jnp.sum(jnp.where(named, share, 0.0), axis=2)
    hit = jnp.any(named, axis=2)
    order = jnp.arange(row_count)
    earlier = order[None, :] < order[:, None]
    slot = jnp.sum((hit[:, None, :] & earlier[None]).astype(jnp.int32), axis=2)
    place = jnp.arange(expert_count, dtype=jnp.int32)[:, None] * SLOT + slot
    code = jnp.where(hit & (slot < SLOT), place, -1)
    targets = jnp.arange(capacity, dtype=jnp.int32)
    picks = [
        (code[:, a:b].reshape(-1)[None, :] == targets[:, None]).astype(jnp.bfloat16)
        for a, b in zip(edges, edges[1:])
    ]
    both_part, both_send = expert_halves(
        picks, gathered, gate_proj, up_proj, [sends[0, 0]]
    )
    both_own, both_recv = exchange(both_part, both_send)

    send_part(0, 1, [both_send])
    send_part(1, 0, [sends[0, 1], recv[0, 0]])

    both = both_own + behind(both_recv, sends[1, 0]).astype(jnp.float32)
    hidden_width = gate_proj.shape[2]
    hidden = (jax.nn.silu(both[:, :hidden_width]) * both[:, hidden_width:]).astype(jnp.bfloat16)
    expert_out = jnp.dot(hidden, down_proj[0], preferred_element_type=jnp.float32).astype(
        jnp.bfloat16
    )

    def returned(a, b):
        picker = (code[a:b].reshape(-1)[:, None] == targets[None, :]).astype(jnp.bfloat16)
        rows = jnp.dot(picker, expert_out, preferred_element_type=jnp.float32)
        return rows * share[a:b].reshape(-1)[:, None]

    send_part(1, 1, [sends[1, 0], recv[0, 1]])

    half = expert_count // 2
    moe_send = returned(half, expert_count).astype(jnp.bfloat16)

    moe_rows = moe_send.shape[0]
    mask = scatter_masks()[0]
    moe_keep, moe_next = halves(
        add_swapped(returned(0, half), moe_send, mask, []), [moe_rows // 2]
    )

    def rebuild(h, c, total, want, after):
        start, last = cuts[h][c], c == LASTS[h]
        return decode(
            own[h, c], recv[h, c], enc_bias, clamp_pick, want, dec_weight, start, total, last, after
        )

    part = rebuild(0, 1, None, clamp_want, [sends[1, 1]])
    keep, send = rebuild(0, 0, part, clamp_want, [recv[1, 0], moe_next])
    masks = scatter_masks()
    groups = [keep.shape[0] - clamp_count // 2, clamp_count // 2]
    first_keep, first_next = halves(
        add_swapped(keep, send, masks[0], []), [g // 2 for g in groups]
    )
    part = rebuild(1, 0, None, None, [first_next, moe_next])
    first_keep, first_next = halves(
        add_swapped(first_keep, first_next, masks[1], [part]), [g // 4 for g in groups]
    )
    last_keep, last_send = rebuild(1, 1, part, None, [first_next])
    moe_keep, moe_next = halves(
        add_swapped(moe_keep, moe_next, masks[1], [last_send]), [moe_rows // 4]
    )
    second_keep, second_next = halves(
        add_swapped(last_keep, last_send, masks[0], []), [last_keep.shape[0] // 2]
    )
    third_keep, third_next = halves(
        add_swapped(second_keep, second_next, masks[1], []), [last_keep.shape[0] // 4]
    )
    first = scatter_steps(first_keep, first_next, groups, 2, {2: [last_send], 3: [second_next]})
    rows_own = first[SPLIT[0] :, :width].astype(jnp.bfloat16)
    rows_dec = gather_blocks(rows_own)
    moe_out = scatter_steps(moe_keep, moe_next, [moe_rows], 2, {2: [second_next]})
    second = scatter_steps(third_keep, third_next, [last_keep.shape[0]], 2, {})
    summed = jnp.concatenate([first[: SPLIT[0]], second], axis=0)
    chosen = summed[:, width : width + clamp_count]
    change = clamp_values.astype(jnp.float32)[None, :] - chosen
    change = jnp.dot(change, turn.T.astype(jnp.float32), precision=lax.Precision.HIGHEST)
    shift = jnp.dot(change, rows_dec.astype(jnp.float32), precision=lax.Precision.HIGHEST)
    error_term = moe_out - summed[:, :width] - dec_bias
    steered = moe_out + shift
    return (error_term, steered)


def solution(mesh):
    placed = (
        P("exp", "feat"),
        P("exp", None),
        P("exp", None),
        P("exp", "feat", None),
        P("exp", "feat", None),
        P("exp", None, "feat"),
        P("feat", "exp"),
        P("exp"),
        P("exp", "feat"),
        P("feat"),
        P(),
        P(),
    )
    return jax.shard_map(
        local,
        mesh=mesh,
        in_specs=placed,
        out_specs=(P("exp", "feat"), P("exp", "feat")),
        check_vma=False,
    )
```
